32 devices in a mesh: groups: 2 (over y), epoch: 4 (over x, core), tile: 4 (over z).
Axes of the slice: x: 2, y: 2, z: 4, core: 2. Of those that a mesh axis runs over, the one named last changes fastest.
Arguments:
- east_velocity: float32 [256, 16, 2048], P('epoch', ('groups', 'tile')), parts along dimension 1, may hold values from -6 to 6
- up_velocity: float32 [256, 16, 2048], P('epoch', ('groups', 'tile')), parts along dimension 1, may hold values from -6 to 6
- metric_table: float32 [64], replicated, may hold values from 1 to 3
- lat_index: int32 [16], P(('groups', 'tile')), parts along dimension 0, may hold values from 0 to 63
- coherent: int32 [16, 2048], P(('groups', 'tile'), 'epoch'), parts along dimension 0, may hold values 0 or 1
Outputs:
- rfactor: float32 [512, 256], P('groups'), parts along dimension 0
- scores: float32 [3, 256, 16, 2048], P(None, None, ('groups', 'tile'), 'epoch'), parts along dimension 2
The draws below stay inside these ranges and needn't reach their ends.
There are 2 independent parts, one for each index of `groups`. The reference program is written for one: setup_inputs(seed, part) draws one part's arguments, and reference() takes and returns one part's arrays. A program takes and returns all parts, laid end to end along the dimension named above; an argument that names none is the same for every part. Nothing has to cross between parts.
All inputs are finite; a program needn't handle non-finite values. No bound on the sum of `coherent` on one device may be relied on, other than what follows from the above.
Results may differ from the reference program's by a relative error of at most 0.00013.
Values sent between devices are 32-bit elements; how exact they have to be, the bound alone decides.
A program may use at most 64 MiB of HBM per device.

```python
import math
import jax
import jax.numpy as jnp
from jax import lax

T_SIZE = 256
W = 2048
NLAT = 64
H = 8


def drifting(key, amplitude):
    freq_key, amp_key, phase_key = jax.random.split(key, 3)
    frequency = jax.random.randint(freq_key, (6,), 1, 13).astype(jnp.float32)
    amplitudes = amplitude * jax.random.normal(amp_key, (6, H, W), dtype=jnp.float32)
    phases = jax.random.uniform(phase_key, (6, H, W), jnp.float32, -math.pi, math.pi)
    times = jnp.arange(T_SIZE, dtype=jnp.float32)[:, None, None]
    total = jnp.zeros((T_SIZE, H, W), jnp.float32)
    for which_mode in range(6):
        angle_now = 2.0 * math.pi / T_SIZE * frequency[which_mode] * times + phases[which_mode][None]
        total = total + amplitudes[which_mode][None] * jnp.cos(angle_now)
    return total


def draw_east_velocity(key, part):
    key = jax.random.fold_in(key, 11)
    mode_key, jitter_key = jax.random.split(key)
    jitter = jax.random.normal(jitter_key, (T_SIZE, H, W), dtype=jnp.float32)
    field = jitter + drifting(mode_key, 0.6)
    return jnp.clip(field, -6.0, 6.0)


def draw_up_velocity(key, part):
    key = jax.random.fold_in(key, 23)
    mode_key, jitter_key = jax.random.split(key)
    jitter = jax.random.normal(jitter_key, (T_SIZE, H, W), dtype=jnp.float32)
    field = jitter + drifting(mode_key, 0.6)
    return jnp.clip(field, -6.0, 6.0)


def with_ends(values, own_key, least, top_value):
    longest = values.shape.index(max(values.shape))
    spots = []
    for shift in (0, 1):
        where = [jax.random.randint(jax.random.fold_in(own_key, axis), (), 0, length) for axis, length in enumerate(values.shape)]
        where[longest] = (where[longest] + shift) % values.shape[longest]
        spots.append(tuple(where))
    return values.at[spots[0]].set(least).at[spots[1]].set(top_value)


def setup_inputs(seed: int = 0, part: int = 0) -> dict:
    seeds = jax.random.split(jax.random.key(seed), 6)
    part_splits = jax.random.split(jax.random.fold_in(seeds[5], part), 6)
    return {
        "east_velocity": draw_east_velocity(jax.random.fold_in(jax.random.fold_in(seeds[5], part), 71), part),
        "up_velocity": draw_up_velocity(jax.random.fold_in(jax.random.fold_in(seeds[5], part), 71), part),
        "metric_table": jnp.clip(jnp.exp(jax.random.uniform(seeds[2], (NLAT,), jnp.float32, math.log(1.0), math.log(3.0))), 1.0, 3.0),
        "lat_index": with_ends(jax.random.randint(part_splits[3], (H,), 0, NLAT), jax.random.fold_in(part_splits[3], 1), 0, NLAT - 1).astype(jnp.int32),
        "coherent": with_ends((jax.random.randint(part_splits[4], (H, W), 0, 4) < 3).astype(jnp.int32), jax.random.fold_in(part_splits[4], 1), 0, 1),
    }


def gradients(field):
    padded = jnp.pad(field, ((0, 0), (1, 1), (1, 1)))
    along_x = 0.5 * (padded[:, 1:-1, 2:] - padded[:, 1:-1, :-2])
    along_y = 0.5 * (padded[:, 2:, 1:-1] - padded[:, :-2, 1:-1])
    return (along_x, along_y)

def reference(east_velocity, up_velocity, metric_table, lat_index, coherent):
    metric = metric_table[lat_index][None, :, None]
    east_x, east_y = gradients(east_velocity)
    up_x, up_y = gradients(up_velocity)
    strain = jnp.stack([metric * east_x, east_y, metric * up_x + up_y])
    steps_t = jnp.arange(T_SIZE, dtype=jnp.float32) - jnp.float32((T_SIZE - 1) / 2.0)
    shaped = steps_t[None, :, None, None]
    center = jnp.mean(strain, axis=1, keepdims=True)
    slope = jnp.sum(strain * shaped, axis=1, keepdims=True) / jnp.sum(steps_t * steps_t)
    series = (strain - center - slope * shaped) * coherent.astype(jnp.float32)[None, None]
    gram = jnp.einsum('ktrc,kurc->tu', series, series, precision=lax.Precision.HIGHEST)
    gram = gram / jnp.float32(3 * H * W) + 0.05 * jnp.eye(T_SIZE, dtype=jnp.float32)
    lower = jnp.linalg.cholesky(gram)
    inverse = jax.scipy.linalg.solve_triangular(lower, jnp.eye(T_SIZE, dtype=jnp.float32), lower=True)
    scores = jnp.einsum('tu,kurc->ktrc', inverse, series, precision=lax.Precision.HIGHEST)
    return (jnp.transpose(lower), scores)
```

```python
import jax
import jax.numpy as jnp
from jax import lax
from jax.sharding import PartitionSpec as P

NLAT = 64


def with_halo(block, sides, width):
    for axis, dim in sides:
        count = lax.axis_size(axis)
        forward = [(i, i + 1) for i in range(count - 1)]
        backward = [(target, source) for source, target in forward]
        low = lax.ppermute(
            lax.slice_in_dim(block, block.shape[dim] - width, None, axis=dim), axis, forward
        )
        high = lax.ppermute(lax.slice_in_dim(block, 0, width, axis=dim), axis, backward)
        block = jnp.concatenate([low, block, high], axis=dim)
    return block


def strain_parts(padded, metric):
    east = padded[0]
    up_part = padded[1]
    scale = metric[None, :, None]
    east_x = 0.5 * (east[:, 1:-1, 2:] - east[:, 1:-1, :-2])
    east_y = 0.5 * (east[:, 2:, 1:-1] - east[:, :-2, 1:-1])
    up_x = 0.5 * (up_part[:, 1:-1, 2:] - up_part[:, 1:-1, :-2])
    up_y = 0.5 * (up_part[:, 2:, 1:-1] - up_part[:, :-2, 1:-1])
    return jnp.stack([scale * east_x, east_y, scale * up_x + up_y])


def on_device(east_velocity, up_velocity, metric_table, lat_index, coherent):
    entries = jnp.arange(NLAT, dtype=jnp.int32)
    onehot = (lat_index[:, None] == entries[None, :]).astype(jnp.float32)
    metric = jnp.sum(onehot * metric_table[None, :], axis=1)
    velocity = jnp.stack([east_velocity, up_velocity])
    columns = velocity.shape[3]
    rows_local = velocity.shape[2]
    padded = with_halo(velocity, (("tile", 2),), 1)
    padded = jnp.pad(padded, ((0, 0), (0, 0), (0, 0), (1, 1)))
    strain = strain_parts(padded, metric)
    strain = lax.all_to_all(strain, "epoch", split_axis=3, concat_axis=1, tiled=True)
    epochs = strain.shape[1]
    steps_t = jnp.arange(epochs, dtype=jnp.float32) - jnp.float32((epochs - 1) / 2.0)
    shaped = steps_t[None, :, None, None]
    center = jnp.mean(strain, axis=1, keepdims=True)
    slope = jnp.sum(strain * shaped, axis=1, keepdims=True) / jnp.sum(steps_t * steps_t)
    series = (strain - center - slope * shaped) * coherent.astype(jnp.float32)[None, None]
    count = jnp.float32(3 * rows_local * lax.axis_size("tile") * columns)
    local_gram = (
        jnp.einsum("ktrc,kurc->tu", series, series, precision=lax.Precision.HIGHEST) / count
    )
    identity = jnp.eye(epochs, dtype=jnp.float32)
    gram = lax.psum(local_gram, ("epoch", "tile")) + 0.05 * identity
    lower = jnp.linalg.cholesky(gram)
    inverse = jax.scipy.linalg.solve_triangular(lower, identity, lower=True)
    scores = jnp.einsum("tu,kurc->ktrc", inverse, series, precision=lax.Precision.HIGHEST)
    return (jnp.transpose(lower), scores)


def solution(mesh):
    in_specs = (
        P("epoch", ("groups", "tile"), None),
        P("epoch", ("groups", "tile"), None),
        P(),
        P(("groups", "tile")),
        P(("groups", "tile"), "epoch"),
    )
    out_specs = (P("groups", None), P(None, None, ("groups", "tile"), "epoch"))
    return jax.shard_map(
        on_device, mesh=mesh, in_specs=in_specs, out_specs=out_specs, check_vma=False
    )
```

```python
import functools

import jax
import jax.numpy as jnp
from jax import lax
from jax.experimental import pallas as pl
from jax.experimental.pallas import tpu as pltpu
from jax.sharding import PartitionSpec as P

MESH = pl.DeviceIdType.MESH
HIGHEST = lax.Precision.HIGHEST
LANES = 128
LEAF = 32
SUB = 8
VMEM_LIMIT = 48 * 1024 * 1024


def exchange_kernel(
    count_e, count_z, v_ref, edge_ref, buf_ref, col_ref,
    send, recv, edge_send, edge_recv, z_send, z_recv, local,
):
    g, e, z = lax.axis_index("groups"), lax.axis_index("epoch"), lax.axis_index("tile")
    fields, rows, te, columns = v_ref.shape
    wc = columns // count_e
    has_down, has_up = z > 0, z < count_z - 1

    barrier = pltpu.get_barrier_semaphore()
    for d in range(1, count_e):
        pl.semaphore_signal(barrier, inc=1, device_id=(g, (e + d) % count_e, z), device_id_type=MESH)

    @pl.when(has_down)
    def _():
        pl.semaphore_signal(barrier, inc=1, device_id=(g, e, z - 1), device_id_type=MESH)

    @pl.when(has_up)
    def _():
        pl.semaphore_signal(barrier, inc=1, device_id=(g, e, z + 1), device_id_type=MESH)

    neighbours = lax.div(z + count_z - 1, count_z) + lax.div(2 * (count_z - 1) - z, count_z)
    pl.semaphore_wait(barrier, count_e - 1 + neighbours)

    def cols(who):
        return pl.ds(pl.multiple_of(who * wc, LANES), wc)

    def times(who):
        return pl.ds(pl.multiple_of(who * te, 8), te)

    chunks = [(r, f) for r in range(rows) for f in range(fields)]

    def across(d, c):
        r, f = chunks[c]
        to = (e + d) % count_e
        return pltpu.make_async_remote_copy(
            src_ref=v_ref.at[f, r, :, cols(to)],
            dst_ref=buf_ref.at[f, r + 1, times(e), :],
            send_sem=send.at[d, c], recv_sem=recv.at[d, c],
            device_id=(g, to, z), device_id_type=MESH,
        )

    def edges(d):
        to = (e + d) % count_e
        return pltpu.make_async_remote_copy(
            src_ref=edge_ref.at[to], dst_ref=col_ref.at[times(e), :],
            send_sem=edge_send.at[d], recv_sem=edge_recv.at[d],
            device_id=(g, to, z), device_id_type=MESH,
        )

    def beside(d, f, up):
        source = (e + count_e - d) % count_e
        r = rows - 1 if up else 0
        src = v_ref.at[f, r, :, cols(e)] if d == 0 else buf_ref.at[f, r + 1, times(source), :]
        side = 1 if up else 0
        return pltpu.make_async_remote_copy(
            src_ref=src, dst_ref=buf_ref.at[f, 0 if up else rows + 1, times(source), :],
            send_sem=z_send.at[side, d, f], recv_sem=z_recv.at[side, d, f],
            device_id=(g, e, z + 1 if up else z - 1), device_id_type=MESH,
        )

    def forward(d, c):
        r, f = chunks[c]
        if r == 0:
            @pl.when(has_down)
            def _():
                beside(d, f, False).start()
        if r == rows - 1:
            @pl.when(has_up)
            def _():
                beside(d, f, True).start()

    own = []
    for c in range(len(chunks)):
        for d in range(1, count_e):
            across(d, c).start()
        forward(0, c)
        r, f = chunks[c]
        own.append(pltpu.make_async_copy(
            v_ref.at[f, r, :, cols(e)], buf_ref.at[f, r + 1, times(e), :], local.at[c]))
        own[-1].start()
    for d in range(1, count_e):
        edges(d).start()
    own.append(pltpu.make_async_copy(edge_ref.at[e], col_ref.at[times(e), :], local.at[len(chunks)]))
    own[-1].start()

    for c in range(len(chunks)):
        for d in range(1, count_e):
            across(d, c).wait_recv()
            forward(d, c)
    for d in range(1, count_e):
        edges(d).wait()
        for c in range(len(chunks)):
            across(d, c).wait_send()
    for copy in own:
        copy.wait()

    @pl.when(has_down)
    def _():
        for d in range(count_e):
            for f in range(fields):
                beside(d, f, False).wait_send()
                beside(d, f, True).wait_recv()

    @pl.when(has_up)
    def _():
        for d in range(count_e):
            for f in range(fields):
                beside(d, f, True).wait_send()
                beside(d, f, False).wait_recv()


def exchange(velocity, edge, count_e, count_z):
    fields, rows, te, columns = velocity.shape
    wc = columns // count_e
    n = fields * rows
    dma = pltpu.SemaphoreType.DMA
    return pl.pallas_call(
        functools.partial(exchange_kernel, count_e, count_z),
        out_shape=(
            jax.ShapeDtypeStruct((fields, rows + 2, te * count_e, wc), jnp.float32),
            jax.ShapeDtypeStruct((te * count_e, LANES), jnp.float32),
        ),
        in_specs=[pl.BlockSpec(memory_space=pl.ANY)] * 2,
        out_specs=(pl.BlockSpec(memory_space=pl.ANY),) * 2,
        scratch_shapes=[
            dma((count_e, n)), dma((count_e, n)), dma((count_e,)), dma((count_e,)),
            dma((2, count_e, fields)), dma((2, count_e, fields)), dma((n + 1,)),
        ],
        compiler_params=pltpu.CompilerParams(collective_id=0, has_side_effects=True),
        name="exchange",
    )(velocity, edge)


def nt(a, b):
    return lax.dot_general(
        a, b, (((1,), (1,)), ((), ())), precision=HIGHEST, preferred_element_type=jnp.float32)


def series_kernel(count_z, lat_ref, table_ref, coh_ref, buf_ref, col_ref, s_ref, gram_ref):
    z = lax.axis_index("tile")
    _, padded_rows, epochs, wc = buf_ref.shape
    rows = padded_rows - 2
    lane = lax.broadcasted_iota(jnp.int32, (epochs, wc), 1)
    steps = lax.broadcasted_iota(jnp.int32, (epochs, 1), 0).astype(jnp.float32) - (epochs - 1) / 2.0
    squares = epochs * (epochs * epochs - 1) / 12.0

    def along_x(f, r):
        x = buf_ref[f, r + 1]
        at = (f * rows + r) * 2
        right = jnp.where(lane == wc - 1, col_ref[:, at + 1:at + 2], pltpu.roll(x, wc - 1, 1))
        left = jnp.where(lane == 0, col_ref[:, at:at + 1], pltpu.roll(x, 1, 1))
        return 0.5 * (right - left)

    def row(f, i):
        x = buf_ref[f, i]
        if i == 0:
            x = jnp.where(z > 0, x, 0.0)
        if i == rows + 1:
            x = jnp.where(z < count_z - 1, x, 0.0)
        return x

    def along_y(f, r):
        return 0.5 * (row(f, r + 2) - row(f, r))

    total = None
    for r in range(rows):
        m = table_ref[lat_ref[r]]
        mask = coh_ref[r:r + 1, :].astype(jnp.float32)
        for k in range(3):
            if k == 0:
                strain = m * along_x(0, r)
            elif k == 1:
                strain = along_y(0, r)
            else:
                strain = m * along_x(1, r) + along_y(1, r)
            center = jnp.sum(strain, axis=0, keepdims=True) * (1.0 / epochs)
            slope = jnp.sum(strain * steps, axis=0, keepdims=True) * (1.0 / squares)
            series = (strain - center - slope * steps) * mask
            s_ref[k, r] = series
            part = nt(series, series)
            total = part if total is None else total + part
    gram_ref[...] = total


def make_series(lat_index, metric_table, coherent, buf, col, count_z):
    fields, padded_rows, epochs, wc = buf.shape
    smem, vmem = pl.BlockSpec(memory_space=pltpu.SMEM), pl.BlockSpec(memory_space=pltpu.VMEM)
    return pl.pallas_call(
        functools.partial(series_kernel, count_z),
        out_shape=(
            jax.ShapeDtypeStruct((3, padded_rows - 2, epochs, wc), jnp.float32),
            jax.ShapeDtypeStruct((epochs, epochs), jnp.float32),
        ),
        in_specs=[smem, smem, vmem, vmem, vmem],
        out_specs=(vmem, vmem),
        compiler_params=pltpu.CompilerParams(vmem_limit_bytes=VMEM_LIMIT),
        name="series",
    )(lat_index, metric_table, coherent, buf, col)


def reduce_kernel(count_e, count_z, x_ref, o_ref, parts, sums, full, s1, r1, s2, r2, s3, r3):
    g, e, z = lax.axis_index("groups"), lax.axis_index("epoch"), lax.axis_index("tile")
    size = x_ref.shape[0] // count_e

    def rows(who):
        return pl.ds(pl.multiple_of(who * size, 8), size)

    barrier = pltpu.get_barrier_semaphore()
    for d in range(1, count_e):
        pl.semaphore_signal(barrier, inc=1, device_id=(g, (e + d) % count_e, z), device_id_type=MESH)
    for d in range(1, count_z):
        pl.semaphore_signal(barrier, inc=1, device_id=(g, e, (z + d) % count_z), device_id_type=MESH)
    pl.semaphore_wait(barrier, count_e + count_z - 2)

    def scatter(d):
        to = (e + d) % count_e
        return pltpu.make_async_remote_copy(
            src_ref=x_ref.at[rows(to), :], dst_ref=parts.at[d], send_sem=s1.at[d], recv_sem=r1.at[d],
            device_id=(g, to, z), device_id_type=MESH)

    def share(d):
        to = (z + d) % count_z
        return pltpu.make_async_remote_copy(
            src_ref=sums.at[0], dst_ref=sums.at[d], send_sem=s2.at[d], recv_sem=r2.at[d],
            device_id=(g, e, to), device_id_type=MESH)

    def gather(d):
        to = (e + d) % count_e
        return pltpu.make_async_remote_copy(
            src_ref=full.at[rows(e), :], dst_ref=full.at[rows(e), :], send_sem=s3.at[d], recv_sem=r3.at[d],
            device_id=(g, to, z), device_id_type=MESH)

    for d in range(1, count_e):
        scatter(d).start()
    total = x_ref[rows(e), :]
    for d in range(1, count_e):
        scatter(d).wait_recv()
        total = total + parts[d]
    sums[0] = total
    for d in range(1, count_z):
        share(d).start()
    for d in range(1, count_z):
        share(d).wait_recv()
    total = None
    for i in range(count_z):
        part = sums[(z + count_z - i) % count_z]
        total = part if total is None else total + part
    full[rows(e), :] = total
    for d in range(1, count_e):
        gather(d).start()
    for d in range(1, count_e):
        gather(d).wait_recv()
    o_ref[...] = full[...]
    for d in range(1, count_e):
        scatter(d).wait_send()
        gather(d).wait_send()
    for d in range(1, count_z):
        share(d).wait_send()


def reduce_gram(gram, count_e, count_z):
    n = gram.shape[0]
    size = n // count_e
    dma = pltpu.SemaphoreType.DMA
    vmem = pl.BlockSpec(memory_space=pltpu.VMEM)
    return pl.pallas_call(
        functools.partial(reduce_kernel, count_e, count_z),
        out_shape=jax.ShapeDtypeStruct((n, n), jnp.float32),
        in_specs=[vmem],
        out_specs=vmem,
        scratch_shapes=[
            pltpu.VMEM((count_e, size, n), jnp.float32),
            pltpu.VMEM((count_z, size, n), jnp.float32),
            pltpu.VMEM((n, n), jnp.float32),
            dma((count_e,)), dma((count_e,)), dma((count_z,)), dma((count_z,)),
            dma((count_e,)), dma((count_e,)),
        ],
        compiler_params=pltpu.CompilerParams(collective_id=1, has_side_effects=True),
        name="reduce_gram",
    )(gram)


def leaf_inverse(block):
    n = block.shape[0]
    i = lax.broadcasted_iota(jnp.int32, (n, LANES), 0)
    j = lax.broadcasted_iota(jnp.int32, (n, LANES), 1)
    eye = (j == i + n).astype(jnp.float32)
    pad = jnp.zeros((n, LANES - n), jnp.float32)
    work = jnp.concatenate([block, pad], axis=1) + eye
    pivots = jnp.ones((n, LANES), jnp.float32)
    for start in range(0, n, SUB):
        held = [jnp.broadcast_to(work[:, c:c + 1], (n, LANES)) for c in range(start, start + SUB)]
        for c in range(start, start + SUB):
            column = held[c - start]
            pivot = column[c:c + 1, :]
            factor = jnp.where(i > c, column * (1.0 / pivot), 0.0)
            pivots = jnp.where(i == c, pivot, pivots)
            for k in range(c + 1, start + SUB):
                held[k - start] = held[k - start] - factor * held[k - start][c:c + 1, :]
            work = work - factor * work[c:c + 1, :]
    return (work * lax.rsqrt(pivots))[:, n:2 * n]


def scores_kernel(count, s_ref, gram_ref, r_ref, out_ref, work):
    epochs = gram_ref.shape[0]
    rows, wc = s_ref.shape[1], s_ref.shape[3]
    i = lax.broadcasted_iota(jnp.int32, (epochs, epochs), 0)
    j = lax.broadcasted_iota(jnp.int32, (epochs, epochs), 1)
    eye = (i == j).astype(jnp.float32)
    work[:, :epochs] = gram_ref[...] * (1.0 / count) + 0.05 * eye
    work[:, epochs:] = eye
    for start in range(0, epochs, LEAF):
        stop = start + LEAF
        inner = leaf_inverse(work[start:stop, start:stop])
        rows_now = jnp.dot(inner, work[start:stop, :], precision=HIGHEST, preferred_element_type=jnp.float32)
        work[start:stop, :] = rows_now
        if stop < epochs:
            head = rows_now[:, :epochs]
            update = lax.dot_general(
                head, rows_now, (((0,), (0,)), ((), ())), precision=HIGHEST,
                preferred_element_type=jnp.float32)
            work[stop:, :] = work[stop:, :] - update[stop:, :]
    r_ref[...] = jnp.where(i <= j, work[:, :epochs], 0.0)
    whiten = jnp.where(i >= j, work[:, epochs:], 0.0)
    tiles = wc // LANES
    for k in range(3):
        for r in range(rows):
            result = jnp.dot(whiten, s_ref[k, r], precision=HIGHEST, preferred_element_type=jnp.float32)
            for c in range(tiles):
                out_ref[k, pl.ds(c * rows + r, epochs, stride=tiles * rows), :] = result[:, c * LANES:(c + 1) * LANES]


def make_scores(series, gram, count):
    _, rows, epochs, wc = series.shape
    vmem = pl.BlockSpec(memory_space=pltpu.VMEM)
    rfactor, scores = pl.pallas_call(
        functools.partial(scores_kernel, count),
        out_shape=(
            jax.ShapeDtypeStruct((epochs, epochs), jnp.float32),
            jax.ShapeDtypeStruct((3, epochs * rows * wc // LANES, LANES), jnp.float32),
        ),
        in_specs=[vmem, vmem],
        out_specs=(vmem, vmem),
        scratch_shapes=[pltpu.VMEM((epochs, 2 * epochs), jnp.float32)],
        compiler_params=pltpu.CompilerParams(vmem_limit_bytes=VMEM_LIMIT),
        name="scores",
    )(series, gram)
    scores = scores.reshape(3, epochs, wc // LANES, rows, LANES)
    return rfactor, scores.transpose(0, 1, 3, 2, 4).reshape(3, epochs, rows, wc)


def on_device(count_e, count_z, east_velocity, up_velocity, metric_table, lat_index, coherent):
    velocity = jnp.stack([east_velocity, up_velocity]).transpose(0, 2, 1, 3)
    fields, rows, te, columns = velocity.shape
    wc = columns // count_e
    blank = jnp.zeros((fields, rows, te, 1), jnp.float32)
    left = jnp.concatenate([blank, velocity[..., wc - 1:columns - 1:wc]], axis=3)
    right = jnp.concatenate([velocity[..., wc:columns:wc], blank], axis=3)
    edge = jnp.stack([left, right], axis=2).reshape(2 * fields * rows, te, count_e).transpose(2, 1, 0)
    edge = jnp.pad(edge, ((0, 0), (0, 0), (0, LANES - 2 * fields * rows)))
    buf, col = exchange(velocity, edge, count_e, count_z)
    series, gram = make_series(lat_index, metric_table, coherent, buf, col, count_z)
    gram = reduce_gram(gram, count_e, count_z)
    return make_scores(series, gram, 3 * rows * count_z * columns)


def solution(mesh):
    in_specs = (
        P("epoch", ("groups", "tile"), None),
        P("epoch", ("groups", "tile"), None),
        P(),
        P(("groups", "tile")),
        P(("groups", "tile"), "epoch"),
    )
    out_specs = (P("groups", None), P(None, None, ("groups", "tile"), "epoch"))
    return jax.shard_map(
        functools.partial(on_device, mesh.shape["epoch"], mesh.shape["tile"]),
        mesh=mesh, in_specs=in_specs, out_specs=out_specs, check_vma=False,
    )
```

```python
import functools

import jax
import jax.numpy as jnp
from jax import lax
from jax.experimental import pallas as pl
from jax.experimental.pallas import tpu as pltpu
from jax.sharding import PartitionSpec as P

MESH = pl.DeviceIdType.MESH
HIGHEST = lax.Precision.HIGHEST
LANES = 128
LEAF = 32
SUB = 8
PIECES = 2
WINDOW = 2
VMEM_LIMIT = 48 * 1024 * 1024


def exchange_kernel(
    count_e, count_z, v_ref, edge_ref, buf_ref, col_ref,
    send, recv, edge_send, edge_recv, z_send, z_recv, local,
):
    g, e, z = lax.axis_index("groups"), lax.axis_index("epoch"), lax.axis_index("tile")
    fields, rows, te, columns = v_ref.shape
    wc = columns // count_e
    has_down, has_up = z > 0, z < count_z - 1

    barrier = pltpu.get_barrier_semaphore()
    for d in range(1, count_e):
        pl.semaphore_signal(barrier, inc=1, device_id=(g, (e + d) % count_e, z), device_id_type=MESH)

    @pl.when(has_down)
    def _():
        pl.semaphore_signal(barrier, inc=1, device_id=(g, e, z - 1), device_id_type=MESH)

    @pl.when(has_up)
    def _():
        pl.semaphore_signal(barrier, inc=1, device_id=(g, e, z + 1), device_id_type=MESH)

    neighbours = lax.div(z + count_z - 1, count_z) + lax.div(2 * (count_z - 1) - z, count_z)
    pl.semaphore_wait(barrier, count_e - 1 + neighbours)

    def cols(who):
        return pl.ds(pl.multiple_of(who * wc, LANES), wc)

    def times(who):
        return pl.ds(pl.multiple_of(who * te, 8), te)

    chips = count_e // 2
    chip, core = lax.div(e, 2), lax.rem(e, 2)

    def target(d):
        return lax.rem(chip + d // 2, chips) * 2 + lax.rem(core + d % 2, 2)

    def origin(d):
        return lax.rem(chip + chips - d // 2, chips) * 2 + lax.rem(core + d % 2, 2)

    chunks = [(r, f, h) for h in range(PIECES) for f in range(fields) for r in range(rows)]
    piece = te // PIECES

    def some(who, h):
        return pl.ds(pl.multiple_of(who * te + h * piece, 8), piece)

    def across(d, c):
        r, f, h = chunks[c]
        to = target(d)
        return pltpu.make_async_remote_copy(
            src_ref=v_ref.at[f, r, pl.ds(h * piece, piece), cols(to)],
            dst_ref=buf_ref.at[f, r + 1, some(e, h), :],
            send_sem=send.at[d, c], recv_sem=recv.at[d, c],
            device_id=(g, to, z), device_id_type=MESH,
        )

    def edges(d):
        to = target(d)
        return pltpu.make_async_remote_copy(
            src_ref=edge_ref.at[to], dst_ref=col_ref.at[times(e), :],
            send_sem=edge_send.at[d], recv_sem=edge_recv.at[d],
            device_id=(g, to, z), device_id_type=MESH,
        )

    def beside(d, f, h, up):
        r = rows - 1 if up else 0
        where = some(origin(d), h)
        src = v_ref.at[f, r, pl.ds(h * piece, piece), cols(e)] if d == 0 else buf_ref.at[f, r + 1, where, :]
        side = 1 if up else 0
        return pltpu.make_async_remote_copy(
            src_ref=src, dst_ref=buf_ref.at[f, 0 if up else rows + 1, where, :],
            send_sem=z_send.at[side, d, f * PIECES + h], recv_sem=z_recv.at[side, d, f * PIECES + h],
            device_id=(g, e, z + 1 if up else z - 1), device_id_type=MESH,
        )

    def forward(d, c):
        r, f, h = chunks[c]
        if r == 0:
            @pl.when(has_down)
            def _():
                beside(d, f, h, False).start()
        if r == rows - 1:
            @pl.when(has_up)
            def _():
                beside(d, f, h, True).start()

    far = range(2, count_e)
    for c in range(min(WINDOW, len(chunks))):
        for d in far:
            across(d, c).start()
    for d in range(1, count_e):
        edges(d).start()
    for c in range(len(chunks)):
        across(1, c).start()
    for c in range(len(chunks)):
        forward(0, c)
    own = []
    for f in range(fields):
        for r in range(rows):
            own.append(pltpu.make_async_copy(
                v_ref.at[f, r, :, cols(e)], buf_ref.at[f, r + 1, times(e), :], local.at[f * rows + r]))
    own.append(pltpu.make_async_copy(edge_ref.at[e], col_ref.at[times(e), :], local.at[fields * rows]))
    for copy in own:
        copy.start()
    for c in range(len(chunks)):
        across(1, c).wait_recv()
        forward(1, c)
    for c in range(len(chunks)):
        for d in far:
            across(d, c).wait_recv()
            forward(d, c)
            if c + WINDOW < len(chunks):
                across(d, c + WINDOW).start()
    for d in range(1, count_e):
        edges(d).wait()
        for c in range(len(chunks)):
            across(d, c).wait_send()
    for copy in own:
        copy.wait()

    halves = [(d, f, h) for d in range(count_e) for f in range(fields) for h in range(PIECES)]

    @pl.when(has_down)
    def _():
        for d, f, h in halves:
            beside(d, f, h, False).wait_send()
            beside(d, f, h, True).wait_recv()

    @pl.when(has_up)
    def _():
        for d, f, h in halves:
            beside(d, f, h, True).wait_send()
            beside(d, f, h, False).wait_recv()


def exchange(velocity, edge, count_e, count_z):
    fields, rows, te, columns = velocity.shape
    wc = columns // count_e
    n = fields * rows
    dma = pltpu.SemaphoreType.DMA
    return pl.pallas_call(
        functools.partial(exchange_kernel, count_e, count_z),
        out_shape=(
            jax.ShapeDtypeStruct((fields, rows + 2, te * count_e, wc), jnp.float32),
            jax.ShapeDtypeStruct((te * count_e, LANES), jnp.float32),
        ),
        in_specs=[pl.BlockSpec(memory_space=pl.ANY)] * 2,
        out_specs=(pl.BlockSpec(memory_space=pl.ANY),) * 2,
        scratch_shapes=[
            dma((count_e, n * PIECES)), dma((count_e, n * PIECES)), dma((count_e,)), dma((count_e,)),
            dma((2, count_e, fields * PIECES)), dma((2, count_e, fields * PIECES)), dma((n + 1,)),
        ],
        compiler_params=pltpu.CompilerParams(collective_id=0, has_side_effects=True),
        name="exchange",
    )(velocity, edge)


def nt(a, b):
    return lax.dot_general(
        a, b, (((1,), (1,)), ((), ())), precision=HIGHEST, preferred_element_type=jnp.float32)


def series_kernel(
    count_e, count_z, lat_ref, table_ref, coh_ref, buf_ref, col_ref, s_ref, gram_ref,
    packed, parts, sums, s1, r1, s2, r2, s3, r3,
):
    g, e, z = lax.axis_index("groups"), lax.axis_index("epoch"), lax.axis_index("tile")
    barrier = pltpu.get_barrier_semaphore()
    for d in range(1, count_e):
        pl.semaphore_signal(barrier, inc=1, device_id=(g, (e + d) % count_e, z), device_id_type=MESH)
    for d in range(1, count_z):
        pl.semaphore_signal(barrier, inc=1, device_id=(g, e, (z + d) % count_z), device_id_type=MESH)
    _, padded_rows, epochs, wc = buf_ref.shape
    rows = padded_rows - 2
    lane = lax.broadcasted_iota(jnp.int32, (epochs, wc), 1)
    steps = lax.broadcasted_iota(jnp.int32, (epochs, 1), 0).astype(jnp.float32) - (epochs - 1) / 2.0
    squares = epochs * (epochs * epochs - 1) / 12.0

    def along_x(f, r):
        x = buf_ref[f, r + 1]
        at = (f * rows + r) * 2
        right = jnp.where(lane == wc - 1, col_ref[:, at + 1:at + 2], pltpu.roll(x, wc - 1, 1))
        left = jnp.where(lane == 0, col_ref[:, at:at + 1], pltpu.roll(x, 1, 1))
        return 0.5 * (right - left)

    def row(f, i):
        x = buf_ref[f, i]
        if i == 0:
            x = jnp.where(z > 0, x, 0.0)
        if i == rows + 1:
            x = jnp.where(z < count_z - 1, x, 0.0)
        return x

    def along_y(f, r):
        return 0.5 * (row(f, r + 2) - row(f, r))

    total = None
    for r in range(rows):
        m = table_ref[lat_ref[r]]
        mask = coh_ref[r:r + 1, :].astype(jnp.float32)
        for k in range(3):
            if k == 0:
                strain = m * along_x(0, r)
            elif k == 1:
                strain = along_y(0, r)
            else:
                strain = m * along_x(1, r) + along_y(1, r)
            center = jnp.sum(strain, axis=0, keepdims=True) * (1.0 / epochs)
            slope = jnp.sum(strain * steps, axis=0, keepdims=True) * (1.0 / squares)
            series = (strain - center - slope * steps) * mask
            s_ref[k, r] = series
            part = nt(series, series)
            total = part if total is None else total + part
    for at, (bi, bj) in enumerate(packed_blocks(epochs)):
        packed[at * LANES:(at + 1) * LANES, :] = total[bi * LANES:(bi + 1) * LANES, bj * LANES:(bj + 1) * LANES]

    size = packed.shape[0] // count_e

    def rows_of(who):
        return pl.ds(pl.multiple_of(who * size, 8), size)

    pl.semaphore_wait(barrier, count_e + count_z - 2)

    def scatter(d):
        to = (e + d) % count_e
        return pltpu.make_async_remote_copy(
            src_ref=packed.at[rows_of(to), :], dst_ref=parts.at[d], send_sem=s1.at[d], recv_sem=r1.at[d],
            device_id=(g, to, z), device_id_type=MESH)

    def share(d):
        to = (z + d) % count_z
        return pltpu.make_async_remote_copy(
            src_ref=sums.at[0], dst_ref=sums.at[d], send_sem=s2.at[d], recv_sem=r2.at[d],
            device_id=(g, e, to), device_id_type=MESH)

    def gather(d):
        to = (e + d) % count_e
        return pltpu.make_async_remote_copy(
            src_ref=gram_ref.at[rows_of(e), :], dst_ref=gram_ref.at[rows_of(e), :], send_sem=s3.at[d], recv_sem=r3.at[d],
            device_id=(g, to, z), device_id_type=MESH)

    for d in range(1, count_e):
        scatter(d).start()
    total = packed[rows_of(e), :]
    for d in range(1, count_e):
        scatter(d).wait_recv()
        total = total + parts[d]
    sums[0] = total
    for d in range(1, count_z):
        share(d).start()
    for d in range(1, count_z):
        share(d).wait_recv()
    total = None
    for i in range(count_z):
        part = sums[(z + count_z - i) % count_z]
        total = part if total is None else total + part
    gram_ref[rows_of(e), :] = total
    for d in range(1, count_e):
        gather(d).start()
    for d in range(1, count_e):
        gather(d).wait_recv()
    for d in range(1, count_e):
        scatter(d).wait_send()
        gather(d).wait_send()
    for d in range(1, count_z):
        share(d).wait_send()


def make_series(lat_index, metric_table, coherent, buf, col, count_e, count_z):
    fields, padded_rows, epochs, wc = buf.shape
    smem, vmem = pl.BlockSpec(memory_space=pltpu.SMEM), pl.BlockSpec(memory_space=pltpu.VMEM)
    dma = pltpu.SemaphoreType.DMA
    lines = len(packed_blocks(epochs)) * LANES
    return pl.pallas_call(
        functools.partial(series_kernel, count_e, count_z),
        out_shape=(
            jax.ShapeDtypeStruct((3, padded_rows - 2, epochs, wc), jnp.float32),
            jax.ShapeDtypeStruct((lines, LANES), jnp.float32),
        ),
        in_specs=[smem, smem, vmem, vmem, vmem],
        out_specs=(vmem, vmem),
        scratch_shapes=[
            pltpu.VMEM((lines, LANES), jnp.float32),
            pltpu.VMEM((count_e, lines // count_e, LANES), jnp.float32),
            pltpu.VMEM((count_z, lines // count_e, LANES), jnp.float32),
            dma((count_e,)), dma((count_e,)), dma((count_z,)), dma((count_z,)),
            dma((count_e,)), dma((count_e,)),
        ],
        compiler_params=pltpu.CompilerParams(
            collective_id=1, has_side_effects=True, vmem_limit_bytes=VMEM_LIMIT),
        name="series",
    )(lat_index, metric_table, coherent, buf, col)


def leaf_inverse(block):
    n = block.shape[0]
    i = lax.broadcasted_iota(jnp.int32, (n, LANES), 0)
    j = lax.broadcasted_iota(jnp.int32, (n, LANES), 1)
    eye = (j == i + n).astype(jnp.float32)
    pad = jnp.zeros((n, LANES - n), jnp.float32)
    work = jnp.concatenate([block, pad], axis=1) + eye
    pivots = jnp.ones((n, LANES), jnp.float32)
    for start in range(0, n, SUB):
        held = [jnp.broadcast_to(work[:, c:c + 1], (n, LANES)) for c in range(start, start + SUB)]
        for c in range(start, start + SUB):
            column = held[c - start]
            pivot = column[c:c + 1, :]
            factor = jnp.where(i > c, column * (1.0 / pivot), 0.0)
            pivots = jnp.where(i == c, pivot, pivots)
            for k in range(c + 1, start + SUB):
                held[k - start] = held[k - start] - factor * held[k - start][c:c + 1, :]
            work = work - factor * work[c:c + 1, :]
    return (work * lax.rsqrt(pivots))[:, n:2 * n]


def packed_blocks(epochs):
    n = epochs // LANES
    return [(i, j) for i in range(n) for j in range(i, n)]


def scores_kernel(count, s_ref, gram_ref, r_ref, out_ref, work, held, done, fetch, flush):
    epochs = r_ref.shape[0]
    rows, wc = s_ref.shape[1], s_ref.shape[3]
    fetches = [pltpu.make_async_copy(s_ref.at[k], held.at[k], fetch.at[k]) for k in range(3)]
    for copy in fetches:
        copy.start()
    i = lax.broadcasted_iota(jnp.int32, (epochs, epochs), 0)
    j = lax.broadcasted_iota(jnp.int32, (epochs, epochs), 1)
    eye = (i == j).astype(jnp.float32)
    work[:, :epochs] = 0.05 * eye
    work[:, epochs:] = eye
    for at, (bi, bj) in enumerate(packed_blocks(epochs)):
        tile = (pl.ds(bi * LANES, LANES), pl.ds(bj * LANES, LANES))
        work[tile] = work[tile] + gram_ref[at * LANES:(at + 1) * LANES, :] * (1.0 / count)
    for start in range(0, epochs, LEAF):
        stop = start + LEAF
        first = start // LANES * LANES
        last = min(first + LANES, epochs) + epochs
        inner = leaf_inverse(work[start:stop, start:stop])
        now = jnp.dot(inner, work[start:stop, first:last], precision=HIGHEST, preferred_element_type=jnp.float32)
        work[start:stop, first:last] = now
        if stop < epochs:
            base = stop // LANES * LANES
            head = now[:, base - first:epochs - first]
            update = lax.dot_general(
                head, now, (((0,), (0,)), ((), ())), precision=HIGHEST, preferred_element_type=jnp.float32)
            work[stop:, first:last] = work[stop:, first:last] - update[stop - base:, :]
    r_ref[...] = jnp.where(i <= j, work[:, :epochs], 0.0)
    whiten = jnp.where(i >= j, work[:, epochs:], 0.0)
    tiles = wc // LANES
    flushes = []
    for k in range(3):
        fetches[k].wait()
        for r in range(rows):
            result = jnp.dot(whiten, held[k, r], precision=HIGHEST, preferred_element_type=jnp.float32)
            for c in range(tiles):
                done[k, pl.ds(c * rows + r, epochs, stride=tiles * rows), :] = result[:, c * LANES:(c + 1) * LANES]
        flushes.append(pltpu.make_async_copy(done.at[k], out_ref.at[k], flush.at[k]))
        flushes[-1].start()
    for copy in flushes:
        copy.wait()


def make_scores(series, gram, count):
    _, rows, epochs, wc = series.shape
    lines = epochs * rows * wc // LANES
    vmem, anywhere = pl.BlockSpec(memory_space=pltpu.VMEM), pl.BlockSpec(memory_space=pl.ANY)
    rfactor, scores = pl.pallas_call(
        functools.partial(scores_kernel, count),
        out_shape=(
            jax.ShapeDtypeStruct((epochs, epochs), jnp.float32),
            jax.ShapeDtypeStruct((3, lines, LANES), jnp.float32),
        ),
        in_specs=[anywhere, vmem],
        out_specs=(vmem, anywhere),
        scratch_shapes=[
            pltpu.VMEM((epochs, 2 * epochs), jnp.float32),
            pltpu.VMEM(series.shape, jnp.float32),
            pltpu.VMEM((3, lines, LANES), jnp.float32),
            pltpu.SemaphoreType.DMA((3,)),
            pltpu.SemaphoreType.DMA((3,)),
        ],
        compiler_params=pltpu.CompilerParams(vmem_limit_bytes=VMEM_LIMIT),
        name="scores",
    )(series, gram)
    scores = scores.reshape(3, epochs, wc // LANES, rows, LANES)
    return rfactor, scores.transpose(0, 1, 3, 2, 4).reshape(3, epochs, rows, wc)


def on_device(count_e, count_z, east_velocity, up_velocity, metric_table, lat_index, coherent):
    velocity = jnp.stack([east_velocity, up_velocity]).transpose(0, 2, 1, 3)
    fields, rows, te, columns = velocity.shape
    wc = columns // count_e
    blank = jnp.zeros((fields, rows, te, 1), jnp.float32)
    left = jnp.concatenate([blank, velocity[..., wc - 1:columns - 1:wc]], axis=3)
    right = jnp.concatenate([velocity[..., wc:columns:wc], blank], axis=3)
    edge = jnp.stack([left, right], axis=2).reshape(2 * fields * rows, te, count_e).transpose(2, 1, 0)
    edge = jnp.pad(edge, ((0, 0), (0, 0), (0, LANES - 2 * fields * rows)))
    buf, col = exchange(velocity, edge, count_e, count_z)
    series, gram = make_series(lat_index, metric_table, coherent, buf, col, count_e, count_z)
    return make_scores(series, gram, 3 * rows * count_z * columns)


def solution(mesh):
    in_specs = (
        P("epoch", ("groups", "tile"), None),
        P("epoch", ("groups", "tile"), None),
        P(),
        P(("groups", "tile")),
        P(("groups", "tile"), "epoch"),
    )
    out_specs = (P("groups", None), P(None, None, ("groups", "tile"), "epoch"))
    return jax.shard_map(
        functools.partial(on_device, mesh.shape["epoch"], mesh.shape["tile"]),
        mesh=mesh, in_specs=in_specs, out_specs=out_specs, check_vma=False,
    )
```

```python
import functools

import jax
import jax.numpy as jnp
from jax import lax
from jax.experimental import pallas as pl
from jax.experimental.pallas import tpu as pltpu
from jax.sharding import PartitionSpec as P

MESH = pl.DeviceIdType.MESH
HIGHEST = lax.Precision.HIGHEST
LANES = 128
LEAF = 64
SUB = 16
PIECES = 2
WINDOW = 8
VMEM_LIMIT = 48 * 1024 * 1024


def exchange_kernel(
    count_e, count_z, v_ref, edge_ref, buf_ref, col_ref,
    send, recv, edge_send, edge_recv, z_send, z_recv, local,
):
    g, e, z = lax.axis_index("groups"), lax.axis_index("epoch"), lax.axis_index("tile")
    fields, rows, te, columns = v_ref.shape
    wc = columns // count_e
    has_down, has_up = z > 0, z < count_z - 1

    barrier = pltpu.get_barrier_semaphore()
    for d in range(1, count_e):
        pl.semaphore_signal(barrier, inc=1, device_id=(g, (e + d) % count_e, z), device_id_type=MESH)

    @pl.when(has_down)
    def _():
        pl.semaphore_signal(barrier, inc=1, device_id=(g, e, z - 1), device_id_type=MESH)

    @pl.when(has_up)
    def _():
        pl.semaphore_signal(barrier, inc=1, device_id=(g, e, z + 1), device_id_type=MESH)

    neighbours = lax.div(z + count_z - 1, count_z) + lax.div(2 * (count_z - 1) - z, count_z)
    pl.semaphore_wait(barrier, count_e - 1 + neighbours)

    def cols(who):
        return pl.ds(pl.multiple_of(who * wc, LANES), wc)

    def times(who):
        return pl.ds(pl.multiple_of(who * te, 8), te)

    chips = count_e // 2
    chip, core = lax.div(e, 2), lax.rem(e, 2)

    def target(d):
        return lax.rem(chip + d // 2, chips) * 2 + lax.rem(core + d % 2, 2)

    def origin(d):
        return lax.rem(chip + chips - d // 2, chips) * 2 + lax.rem(core + d % 2, 2)

    chunks = [(r, f, h) for h in range(PIECES) for f in range(fields) for r in range(rows)]
    piece = te // PIECES

    def some(who, h):
        return pl.ds(pl.multiple_of(who * te + h * piece, 8), piece)

    def across(d, c):
        r, f, h = chunks[c]
        to = target(d)
        return pltpu.make_async_remote_copy(
            src_ref=v_ref.at[f, r, pl.ds(h * piece, piece), cols(to)],
            dst_ref=buf_ref.at[f, r + 1, some(e, h), :],
            send_sem=send.at[d, c], recv_sem=recv.at[d, c],
            device_id=(g, to, z), device_id_type=MESH,
        )

    def edges(d):
        to = target(d)
        return pltpu.make_async_remote_copy(
            src_ref=edge_ref.at[to], dst_ref=col_ref.at[e],
            send_sem=edge_send.at[d], recv_sem=edge_recv.at[d],
            device_id=(g, to, z), device_id_type=MESH,
        )

    def beside(d, f, h, up):
        r = rows - 1 if up else 0
        where = some(origin(d), h)
        src = v_ref.at[f, r, pl.ds(h * piece, piece), cols(e)] if d == 0 else buf_ref.at[f, r + 1, where, :]
        side = 1 if up else 0
        return pltpu.make_async_remote_copy(
            src_ref=src, dst_ref=buf_ref.at[f, 0 if up else rows + 1, where, :],
            send_sem=z_send.at[side, d, f * PIECES + h], recv_sem=z_recv.at[side, d, f * PIECES + h],
            device_id=(g, e, z + 1 if up else z - 1), device_id_type=MESH,
        )

    def forward(d, c):
        r, f, h = chunks[c]
        if r == 0:
            @pl.when(has_down)
            def _():
                beside(d, f, h, False).start()
        if r == rows - 1:
            @pl.when(has_up)
            def _():
                beside(d, f, h, True).start()

    far = range(2, count_e)
    for c in range(min(WINDOW, len(chunks))):
        for d in far:
            across(d, c).start()
    for d in range(1, count_e):
        edges(d).start()
    for c in range(len(chunks)):
        across(1, c).start()
    for c in range(len(chunks)):
        forward(0, c)
    own = []
    for f in range(fields):
        for r in range(rows):
            own.append(pltpu.make_async_copy(
                v_ref.at[f, r, :, cols(e)], buf_ref.at[f, r + 1, times(e), :], local.at[f * rows + r]))
    own.append(pltpu.make_async_copy(edge_ref.at[e], col_ref.at[e], local.at[fields * rows]))
    for copy in own:
        copy.start()
    for c in range(len(chunks)):
        across(1, c).wait_recv()
        forward(1, c)
    for c in range(len(chunks)):
        for d in far:
            across(d, c).wait_recv()
            forward(d, c)
            if c + WINDOW < len(chunks):
                across(d, c + WINDOW).start()
    for d in range(1, count_e):
        edges(d).wait()
        for c in range(len(chunks)):
            across(d, c).wait_send()
    for copy in own:
        copy.wait()

    halves = [(d, f, h) for d in range(count_e) for f in range(fields) for h in range(PIECES)]

    @pl.when(has_down)
    def _():
        for d, f, h in halves:
            beside(d, f, h, False).wait_send()
            beside(d, f, h, True).wait_recv()

    @pl.when(has_up)
    def _():
        for d, f, h in halves:
            beside(d, f, h, True).wait_send()
            beside(d, f, h, False).wait_recv()


def exchange(velocity, edge, count_e, count_z):
    fields, rows, te, columns = velocity.shape
    wc = columns // count_e
    n = fields * rows
    dma = pltpu.SemaphoreType.DMA
    return pl.pallas_call(
        functools.partial(exchange_kernel, count_e, count_z),
        out_shape=(
            jax.ShapeDtypeStruct((fields, rows + 2, te * count_e, wc), jnp.float32),
            jax.ShapeDtypeStruct(edge.shape, jnp.float32),
        ),
        in_specs=[pl.BlockSpec(memory_space=pl.ANY)] * 2,
        out_specs=(pl.BlockSpec(memory_space=pltpu.VMEM),) * 2,
        scratch_shapes=[
            dma((count_e, n * PIECES)), dma((count_e, n * PIECES)), dma((count_e,)), dma((count_e,)),
            dma((2, count_e, fields * PIECES)), dma((2, count_e, fields * PIECES)), dma((n + 1,)),
        ],
        compiler_params=pltpu.CompilerParams(
            collective_id=0, has_side_effects=True, vmem_limit_bytes=VMEM_LIMIT // 4),
        name="exchange",
    )(velocity, edge)


def nt(a, b):
    return lax.dot_general(
        a, b, (((1,), (1,)), ((), ())), precision=HIGHEST, preferred_element_type=jnp.float32)


def series_kernel(
    count_e, count_z, lat_ref, table_ref, coh_ref, buf_ref, col_ref, s_ref, gram_ref,
    packed, parts, sums, s1, r1, s2, r2, s3, r3,
):
    g, e, z = lax.axis_index("groups"), lax.axis_index("epoch"), lax.axis_index("tile")
    barrier = pltpu.get_barrier_semaphore()
    for d in range(1, count_e):
        pl.semaphore_signal(barrier, inc=1, device_id=(g, (e + d) % count_e, z), device_id_type=MESH)
    for d in range(1, count_z):
        pl.semaphore_signal(barrier, inc=1, device_id=(g, e, (z + d) % count_z), device_id_type=MESH)
    _, padded_rows, epochs, wc = buf_ref.shape
    rows = padded_rows - 2
    lane = lax.broadcasted_iota(jnp.int32, (epochs, wc), 1)
    steps = lax.broadcasted_iota(jnp.int32, (epochs, 1), 0).astype(jnp.float32) - (epochs - 1) / 2.0
    squares = epochs * (epochs * epochs - 1) / 12.0

    te = epochs // count_e
    col = jnp.concatenate([col_ref[source].T[:te, :] for source in range(count_e)], axis=0)

    def along_x(f, r):
        x = buf_ref[f, r + 1]
        at = (f * rows + r) * 2
        right = jnp.where(lane == wc - 1, col[:, at + 1:at + 2], pltpu.roll(x, wc - 1, 1))
        left = jnp.where(lane == 0, col[:, at:at + 1], pltpu.roll(x, 1, 1))
        return 0.5 * (right - left)

    def row(f, i):
        x = buf_ref[f, i]
        if i == 0:
            x = jnp.where(z > 0, x, 0.0)
        if i == rows + 1:
            x = jnp.where(z < count_z - 1, x, 0.0)
        return x

    def along_y(f, r):
        return 0.5 * (row(f, r + 2) - row(f, r))

    total = None
    for r in range(rows):
        m = table_ref[lat_ref[r]]
        mask = coh_ref[r:r + 1, :].astype(jnp.float32)
        for k in range(3):
            if k == 0:
                strain = m * along_x(0, r)
            elif k == 1:
                strain = along_y(0, r)
            else:
                strain = m * along_x(1, r) + along_y(1, r)
            center = jnp.sum(strain, axis=0, keepdims=True) * (1.0 / epochs)
            slope = jnp.sum(strain * steps, axis=0, keepdims=True) * (1.0 / squares)
            series = (strain - center - slope * steps) * mask
            s_ref[k, r] = series
            part = nt(series, series)
            total = part if total is None else total + part
    for at, (bi, bj) in enumerate(packed_blocks(epochs)):
        packed[at * LANES:(at + 1) * LANES, :] = total[bi * LANES:(bi + 1) * LANES, bj * LANES:(bj + 1) * LANES]

    size = packed.shape[0] // count_e

    def rows_of(who):
        return pl.ds(pl.multiple_of(who * size, 8), size)

    pl.semaphore_wait(barrier, count_e + count_z - 2)

    def scatter(d):
        to = (e + d) % count_e
        return pltpu.make_async_remote_copy(
            src_ref=packed.at[rows_of(to), :], dst_ref=parts.at[d], send_sem=s1.at[d], recv_sem=r1.at[d],
            device_id=(g, to, z), device_id_type=MESH)

    def share(d):
        to = (z + d) % count_z
        return pltpu.make_async_remote_copy(
            src_ref=sums.at[0], dst_ref=sums.at[d], send_sem=s2.at[d], recv_sem=r2.at[d],
            device_id=(g, e, to), device_id_type=MESH)

    def gather(d):
        to = (e + d) % count_e
        return pltpu.make_async_remote_copy(
            src_ref=gram_ref.at[rows_of(e), :], dst_ref=gram_ref.at[rows_of(e), :], send_sem=s3.at[d], recv_sem=r3.at[d],
            device_id=(g, to, z), device_id_type=MESH)

    for d in range(1, count_e):
        scatter(d).start()
    total = packed[rows_of(e), :]
    for d in range(1, count_e):
        scatter(d).wait_recv()
        total = total + parts[d]
    sums[0] = total
    for d in range(1, count_z):
        share(d).start()
    for d in range(1, count_z):
        share(d).wait_recv()
    total = None
    for i in range(count_z):
        part = sums[(z + count_z - i) % count_z]
        total = part if total is None else total + part
    gram_ref[rows_of(e), :] = total
    for d in range(1, count_e):
        gather(d).start()
    for d in range(1, count_e):
        gather(d).wait_recv()
    for d in range(1, count_e):
        scatter(d).wait_send()
        gather(d).wait_send()
    for d in range(1, count_z):
        share(d).wait_send()


def make_series(lat_index, metric_table, coherent, buf, col, count_e, count_z):
    fields, padded_rows, epochs, wc = buf.shape
    smem, vmem = pl.BlockSpec(memory_space=pltpu.SMEM), pl.BlockSpec(memory_space=pltpu.VMEM)
    dma = pltpu.SemaphoreType.DMA
    lines = len(packed_blocks(epochs)) * LANES
    return pl.pallas_call(
        functools.partial(series_kernel, count_e, count_z),
        out_shape=(
            jax.ShapeDtypeStruct((3, padded_rows - 2, epochs, wc), jnp.float32),
            jax.ShapeDtypeStruct((lines, LANES), jnp.float32),
        ),
        in_specs=[smem, smem, vmem, vmem, vmem],
        out_specs=(vmem, vmem),
        scratch_shapes=[
            pltpu.VMEM((lines, LANES), jnp.float32),
            pltpu.VMEM((count_e, lines // count_e, LANES), jnp.float32),
            pltpu.VMEM((count_z, lines // count_e, LANES), jnp.float32),
            dma((count_e,)), dma((count_e,)), dma((count_z,)), dma((count_z,)),
            dma((count_e,)), dma((count_e,)),
        ],
        compiler_params=pltpu.CompilerParams(
            collective_id=1, has_side_effects=True, vmem_limit_bytes=VMEM_LIMIT // 2),
        name="series",
    )(lat_index, metric_table, coherent, buf, col)


def leaf_inverse(block):
    n = block.shape[0]
    i = lax.broadcasted_iota(jnp.int32, (n, LANES), 0)
    j = lax.broadcasted_iota(jnp.int32, (n, LANES), 1)
    eye = (j == i + n).astype(jnp.float32)
    pad = jnp.zeros((n, LANES - n), jnp.float32)
    work = jnp.concatenate([block, pad], axis=1) + eye
    pivots = jnp.ones((n, LANES), jnp.float32)
    for start in range(0, n, SUB):
        held = [jnp.broadcast_to(work[:, c:c + 1], (n, LANES)) for c in range(start, start + SUB)]
        for c in range(start, start + SUB):
            column = held[c - start]
            pivot = column[c:c + 1, :]
            factor = jnp.where(i > c, column * (1.0 / pivot), 0.0)
            pivots = jnp.where(i == c, pivot, pivots)
            for k in range(c + 1, start + SUB):
                held[k - start] = held[k - start] - factor * held[k - start][c:c + 1, :]
            work = work - factor * work[c:c + 1, :]
    return (work * lax.rsqrt(pivots))[:, n:2 * n]


def packed_blocks(epochs):
    n = epochs // LANES
    return [(i, j) for i in range(n) for j in range(i, n)]


def scores_kernel(count, s_ref, gram_ref, r_ref, out_ref, work, held, done, fetch, flush):
    epochs = r_ref.shape[0]
    rows, wc = s_ref.shape[1], s_ref.shape[3]
    fetches = [pltpu.make_async_copy(s_ref.at[k], held.at[k], fetch.at[k]) for k in range(3)]
    for copy in fetches:
        copy.start()
    i = lax.broadcasted_iota(jnp.int32, (epochs, epochs), 0)
    j = lax.broadcasted_iota(jnp.int32, (epochs, epochs), 1)
    eye = (i == j).astype(jnp.float32)
    work[:, :epochs] = 0.05 * eye
    work[:, epochs:] = eye
    for at, (bi, bj) in enumerate(packed_blocks(epochs)):
        tile = (pl.ds(bi * LANES, LANES), pl.ds(bj * LANES, LANES))
        work[tile] = work[tile] + gram_ref[at * LANES:(at + 1) * LANES, :] * (1.0 / count)
    for start in range(0, epochs, LEAF):
        stop = start + LEAF
        first = start // LANES * LANES
        last = min(first + LANES, epochs) + epochs
        inner = leaf_inverse(work[start:stop, start:stop])
        now = jnp.dot(inner, work[start:stop, first:last], precision=HIGHEST, preferred_element_type=jnp.float32)
        work[start:stop, first:last] = now
        if stop < epochs:
            base = stop // LANES * LANES
            head = now[:, base - first:epochs - first]
            update = lax.dot_general(
                head, now, (((0,), (0,)), ((), ())), precision=HIGHEST, preferred_element_type=jnp.float32)
            work[stop:, first:last] = work[stop:, first:last] - update[stop - base:, :]
    r_ref[...] = jnp.where(i <= j, work[:, :epochs], 0.0)
    whiten = jnp.where(i >= j, work[:, epochs:], 0.0)
    tiles = wc // LANES
    flushes = []
    for k in range(3):
        fetches[k].wait()
        for r in range(rows):
            result = jnp.dot(whiten, held[k, r], precision=HIGHEST, preferred_element_type=jnp.float32)
            for c in range(tiles):
                done[k, pl.ds(c * rows + r, epochs, stride=tiles * rows), :] = result[:, c * LANES:(c + 1) * LANES]
        flushes.append(pltpu.make_async_copy(done.at[k], out_ref.at[k], flush.at[k]))
        flushes[-1].start()
    for copy in flushes:
        copy.wait()


def make_scores(series, gram, count):
    _, rows, epochs, wc = series.shape
    lines = epochs * rows * wc // LANES
    vmem, anywhere = pl.BlockSpec(memory_space=pltpu.VMEM), pl.BlockSpec(memory_space=pl.ANY)
    rfactor, scores = pl.pallas_call(
        functools.partial(scores_kernel, count),
        out_shape=(
            jax.ShapeDtypeStruct((epochs, epochs), jnp.float32),
            jax.ShapeDtypeStruct((3, lines, LANES), jnp.float32),
        ),
        in_specs=[anywhere, vmem],
        out_specs=(vmem, anywhere),
        scratch_shapes=[
            pltpu.VMEM((epochs, 2 * epochs), jnp.float32),
            pltpu.VMEM(series.shape, jnp.float32),
            pltpu.VMEM((3, lines, LANES), jnp.float32),
            pltpu.SemaphoreType.DMA((3,)),
            pltpu.SemaphoreType.DMA((3,)),
        ],
        compiler_params=pltpu.CompilerParams(vmem_limit_bytes=VMEM_LIMIT),
        name="scores",
    )(series, gram)
    scores = scores.reshape(3, epochs, wc // LANES, rows, LANES)
    return rfactor, scores.transpose(0, 1, 3, 2, 4).reshape(3, epochs, rows, wc)


def on_device(count_e, count_z, east_velocity, up_velocity, metric_table, lat_index, coherent):
    velocity = jnp.stack([east_velocity, up_velocity]).transpose(0, 2, 1, 3)
    fields, rows, te, columns = velocity.shape
    wc = columns // count_e
    blank = jnp.zeros((fields, rows, te, 1), jnp.float32)
    left = jnp.concatenate([blank, velocity[..., wc - 1:columns - 1:wc]], axis=3)
    right = jnp.concatenate([velocity[..., wc:columns:wc], blank], axis=3)
    edge = jnp.stack([left, right], axis=2).reshape(2 * fields * rows, te, count_e).transpose(2, 0, 1)
    edge = jnp.pad(edge, ((0, 0), (0, 0), (0, -te % LANES)))
    buf, col = exchange(velocity, edge, count_e, count_z)
    series, gram = make_series(lat_index, metric_table, coherent, buf, col, count_e, count_z)
    return make_scores(series, gram, 3 * rows * count_z * columns)


def solution(mesh):
    in_specs = (
        P("epoch", ("groups", "tile"), None),
        P("epoch", ("groups", "tile"), None),
        P(),
        P(("groups", "tile")),
        P(("groups", "tile"), "epoch"),
    )
    out_specs = (P("groups", None), P(None, None, ("groups", "tile"), "epoch"))
    return jax.shard_map(
        functools.partial(on_device, mesh.shape["epoch"], mesh.shape["tile"]),
        mesh=mesh, in_specs=in_specs, out_specs=out_specs, check_vma=False,
    )
```
